512 devices in a mesh: rows: 16 (over z, core), vars: 32 (over x, y).
Axes of the slice: x: 4, y: 8, z: 8, core: 2. Of those that a mesh axis runs over, the one named last changes fastest.
Arguments:
- matrix: float32 [16384, 16384], P('rows', 'vars'), may hold values from -0.4 to 0.4
- barrier: float32 [16384], P('vars'), may hold values from 0.05 to 20
- panel_index: int32 [1], replicated, may hold values from 0 to 15
- row_offset: int32 [1], replicated, may hold values from 0 to 511
Outputs:
- factor_rows: float32 [16384, 512], P(('rows', 'vars'))
The draws below stay inside these ranges and needn't reach their ends.
All inputs are finite; a program needn't handle non-finite values.
Results may differ from the reference program's by a relative error of at most 0.000092.
Values sent between devices are 32-bit elements; how exact they have to be, the bound alone decides.
No kernel may reach another device: no remote copies, remote signals or barrier semaphores. Data moves between devices by JAX's collectives and lax.ppermute only.
A program may use at most 64 MiB of HBM per device.

```python
import math
import jax
import jax.numpy as jnp
from jax import lax

NWIN = 16384
PANEL = 512
MROWS = 16384


def block_levels(stream_key, shape, cuts, smallest, top_value):
    level, own = 1.0, jax.random.fold_in(stream_key, 6)
    for position, parts in cuts:
        steps = jnp.exp(jax.random.uniform(jax.random.fold_in(own, position), (parts,), jnp.float32, smallest / len(cuts), top_value / len(cuts)))
        level = level * jnp.repeat(steps, shape[position] // parts).reshape([-1 if axis == position else 1 for axis in range(len(shape))])
    return level


def bell_draw(stream_key, extent, deviation, limit, cuts=(), kind=jnp.bfloat16):
    values = jax.random.normal(stream_key, extent, jnp.float32) * deviation
    if len(cuts) > 0:
        values = block_levels(stream_key, extent, cuts, -0.22, 0.18) * values
    return jnp.clip(values, min=-limit, max=limit).astype(kind)


def setup_inputs(seed: int = 0) -> dict:
    key_of = jax.random.split(jax.random.key(seed), 5)
    return {
        "matrix": bell_draw(key_of[0], (MROWS, NWIN), (6.4 / NWIN ** 0.5), 0.4, ((0, 16), (1, 32)), jnp.float32),
        "barrier": jnp.clip(jnp.exp(math.log(20.0) - 5.9914645 * jax.random.uniform(key_of[1], (NWIN,), jnp.float32) ** block_levels(key_of[1], (NWIN,), ((0, 32),), -0.2, 0.2)), 0.05, 20.0),
        "panel_index": jax.random.randint(key_of[2], (1,), 0, MROWS // (2 * PANEL)).astype(jnp.int32),
        "row_offset": jax.random.randint(key_of[3], (1,), 0, PANEL).astype(jnp.int32),
    }


def reference(matrix, barrier, panel_index, row_offset):
    first = (panel_index[0] * PANEL + row_offset[0]).astype(jnp.int32)
    picked = lax.dynamic_slice_in_dim(matrix, first, PANEL, 0)
    scaled = picked * barrier[None, :]
    normal = lax.dot_general(matrix.astype(jnp.float32), scaled.astype(jnp.float32), (((1,), (1,)), ((), ())), precision=lax.Precision.HIGHEST, preferred_element_type=jnp.float32)
    row_ids = jnp.arange(MROWS, dtype=jnp.int32)
    col_ids = jnp.arange(PANEL, dtype=jnp.int32)
    normal = normal + (row_ids[:, None] == first + col_ids[None, :]).astype(normal.dtype)
    diag_block = lax.dynamic_slice_in_dim(normal, first, PANEL, 0)
    lower = jnp.linalg.cholesky(diag_block)
    identity = jnp.eye(PANEL, dtype=normal.dtype)
    inverse = jax.scipy.linalg.solve_triangular(lower, identity, lower=True)
    result = lax.dot_general(normal.astype(jnp.float32), inverse.astype(jnp.float32), (((1,), (1,)), ((), ())), precision=lax.Precision.HIGHEST, preferred_element_type=jnp.float32)
    trailing = (row_ids >= first)[:, None]
    return jnp.where(trailing, result, jnp.zeros_like(result))
```

```python
import functools

import jax
import jax.numpy as jnp
import numpy as np
from jax import lax
from jax.experimental import pallas as pl
from jax.experimental.pallas import tpu as pltpu
from jax.sharding import Mesh
from jax.sharding import PartitionSpec as P

PANEL = 512
BLOCK = 128
GROUP = 8
HIGHEST = lax.Precision.HIGHEST


def product(x, y, dims, precision=HIGHEST):
    return lax.dot_general(
        x, y, (dims, ((), ())), precision=precision, preferred_element_type=jnp.float32
    )


def base_inverse(slabs):
    slabs = list(slabs)
    count = len(slabs)
    n = count * 8
    lane = lax.broadcasted_iota(jnp.int32, (8, n), 1)
    sub = lax.broadcasted_iota(jnp.int32, (8, n), 0)
    for j in range(0, n, GROUP):
        s, o = j // 8, j % 8
        top = slabs[s]
        pivots = [jnp.broadcast_to(top[o + t : o + t + 1, :], (8, n)) for t in range(GROUP)]
        a = [
            [
                jnp.broadcast_to(pivots[t][:, j + u : j + u + 1], (8, n)) if u >= t else None
                for u in range(GROUP)
            ]
            for t in range(GROUP)
        ]
        recip = []
        mult = [[None] * GROUP for _ in range(GROUP)]
        for t in range(GROUP):
            recip.append(1.0 / a[t][t])
            for u in range(t + 1, GROUP):
                mult[u][t] = a[t][u] * recip[t]
            for u in range(t + 1, GROUP):
                for w in range(u, GROUP):
                    a[u][w] = a[u][w] - mult[u][t] * a[t][w]
        inside = (lane >= j) & (lane < j + GROUP)
        full = []
        for t in range(GROUP):
            p = jnp.where(inside, jnp.where(lane == j + t, 1.0, 0.0), pivots[t])
            for u in range(t):
                p = p - mult[t][u] * full[u]
            full.append(p)
        for q in range(s, count):
            cur = slabs[q]
            new = jnp.where(inside, 0.0, cur)
            scaled = []
            for t in range(GROUP):
                c = jnp.broadcast_to(cur[:, j + t : j + t + 1], (8, n))
                for u in range(t):
                    c = c - scaled[u] * a[u][t]
                scaled.append(c * recip[t])
            for t in range(GROUP):
                new = new - scaled[t] * full[t]
            if q == s:
                new = jnp.where(sub >= o + GROUP, new, cur)
                for t in range(GROUP):
                    new = jnp.where(sub == o + t, full[t] * lax.rsqrt(a[t][t]), new)
            slabs[q] = new
    return slabs


def factor_kernel(core_ref, own_ref, other_ref, inv_ref, work):
    n = PANEL
    half = n // 2
    at_own = pl.multiple_of(core_ref[0] * half, half)
    at_other = pl.multiple_of((1 - core_ref[0]) * half, half)
    work[pl.ds(at_own, half), :] = own_ref[...]
    work[pl.ds(at_other, half), :] = other_ref[...]
    inv_ref[...] = jnp.zeros_like(inv_ref)
    keep = lax.broadcasted_iota(jnp.int32, (BLOCK, BLOCK), 0) >= lax.broadcasted_iota(
        jnp.int32, (BLOCK, BLOCK), 1
    )

    def step(k, _):
        at = pl.multiple_of(k * BLOCK, BLOCK)
        block = work[pl.ds(at, BLOCK), pl.ds(at, BLOCK)]
        slabs = base_inverse([block[8 * q : 8 * q + 8, :] for q in range(BLOCK // 8)])
        small = jnp.where(keep, jnp.concatenate(slabs, axis=0), 0.0)
        below = lax.broadcasted_iota(jnp.int32, (n, BLOCK), 0) >= at + BLOCK
        panel = jnp.where(below, product(work[:, pl.ds(at, BLOCK)], small, ((1,), (1,))), 0.0)
        work[...] = work[...] - product(panel, panel, ((1,), (1,)))
        ident = (
            lax.broadcasted_iota(jnp.int32, (BLOCK, n), 1)
            == at + lax.broadcasted_iota(jnp.int32, (BLOCK, n), 0)
        ).astype(jnp.float32)
        done = product(small, inv_ref[pl.ds(at, BLOCK), :] + ident, ((1,), (0,)))
        inv_ref[pl.ds(at, BLOCK), :] = done
        inv_ref[...] = inv_ref[...] - product(panel, done, ((1,), (0,)))
        return 0

    lax.fori_loop(0, n // BLOCK, step, 0)


def factor_inverse(core, own, other):
    vmem = pl.BlockSpec(memory_space=pltpu.VMEM)
    return pl.pallas_call(
        factor_kernel,
        out_shape=jax.ShapeDtypeStruct((PANEL, PANEL), jnp.float32),
        in_specs=[pl.BlockSpec(memory_space=pltpu.SMEM), vmem, vmem],
        out_specs=vmem,
        scratch_shapes=[pltpu.VMEM((PANEL, PANEL), jnp.float32)],
        compiler_params=pltpu.CompilerParams(vmem_limit_bytes=32 * 1024 * 1024),
    )(core.reshape(1), own, other)


def swap(x):
    return lax.ppermute(x, "c", [(0, 1), (1, 0)])


def body(matrix, barrier, panel_index, row_offset):
    nz, nx, ny = lax.axis_size("z"), lax.axis_size("x"), lax.axis_size("y")
    z, c, x, y = (lax.axis_index(name) for name in ("z", "c", "x", "y"))
    rows_here = matrix.shape[0]
    half = PANEL // 2
    chunk = half // nz
    first = panel_index[0] * PANEL + row_offset[0]
    own_first = (2 * z + c) * rows_here
    wanted = first + jnp.arange(PANEL, dtype=jnp.int32) - own_first
    inside = (wanted >= 0) & (wanted < rows_here)
    picked = jnp.where(
        inside[:, None], jnp.take(matrix, jnp.clip(wanted, 0, rows_here - 1), axis=0), 0.0
    )
    mine = lax.dynamic_slice_in_dim(picked, c * half, half, 0)
    theirs = lax.dynamic_slice_in_dim(picked, (1 - c) * half, half, 0)
    mine = mine + swap(theirs)
    part = lax.all_to_all(mine.reshape(nz, chunk, -1), "z", 0, 0, tiled=True).sum(0)
    gathered = lax.all_to_all(
        jnp.broadcast_to(part[None], (nz,) + part.shape), "z", 0, 0, tiled=True
    ).reshape(half, -1)
    facing = swap(gathered)
    low = jnp.where(c == 0, gathered, facing)
    high = jnp.where(c == 0, facing, gathered)
    panel = jnp.concatenate([low, high], axis=0)
    scaled = panel * barrier[None, :]
    local = product(matrix, scaled, ((1,), (1,)), lax.Precision.HIGH)
    partial = product(part, scaled, ((1,), (1,)))
    partial, local = lax.optimization_barrier((partial, local))
    row = lax.all_to_all(partial.reshape(chunk, 1, PANEL), ("x", "y"), 0, 0, tiled=True).sum(0)
    row_id = half * c + chunk * z + ny * x + y
    row = row + (jnp.arange(PANEL, dtype=jnp.int32) == row_id).astype(jnp.float32)[None, :]
    own = lax.all_to_all(
        jnp.broadcast_to(row[None], (nz * nx * ny, 1, PANEL)), ("z", "x", "y"), 0, 0, tiled=True
    ).reshape(half, PANEL)
    other = swap(own)
    summed = lax.psum_scatter(local, "x", scatter_dimension=0, tiled=True)
    own, other, summed = lax.optimization_barrier((own, other, summed))
    summed = lax.psum_scatter(summed, "y", scatter_dimension=0, tiled=True)
    inverse = factor_inverse(c, own, other)
    share_rows = summed.shape[0]
    ids = own_first + (ny * x + y) * share_rows + jnp.arange(share_rows, dtype=jnp.int32)
    cols = jnp.arange(PANEL, dtype=jnp.int32)
    normal = summed + (ids[:, None] == first + cols[None, :]).astype(jnp.float32)
    result = product(normal, inverse, ((1,), (1,)))
    return jnp.where((ids >= first)[:, None], result, 0.0)


def solution(mesh):
    devices = np.asarray(mesh.devices).reshape(8, 2, 4, 8)
    split = Mesh(devices, ("z", "c", "x", "y"))
    return jax.shard_map(
        body,
        mesh=split,
        in_specs=(P(("z", "c"), ("x", "y")), P(("x", "y")), P(), P()),
        out_specs=P(("z", "c", "x", "y"), None),
        check_vma=False,
    )
```

```python
import functools

import jax
import jax.numpy as jnp
import numpy as np
from jax import lax
from jax.experimental import pallas as pl
from jax.experimental.pallas import tpu as pltpu
from jax.sharding import Mesh
from jax.sharding import PartitionSpec as P

PANEL = 512
BLOCK = 128
GROUP = 8
HIGHEST = lax.Precision.HIGHEST


def product(x, y, dims, precision=HIGHEST):
    return lax.dot_general(
        x, y, (dims, ((), ())), precision=precision, preferred_element_type=jnp.float32
    )


def base_inverse(slabs):
    slabs = list(slabs)
    count = len(slabs)
    n = count * 8
    lane = lax.broadcasted_iota(jnp.int32, (8, n), 1)
    sub = lax.broadcasted_iota(jnp.int32, (8, n), 0)
    for j in range(0, n, GROUP):
        s, o = j // 8, j % 8
        top = slabs[s]
        pivots = [jnp.broadcast_to(top[o + t : o + t + 1, :], (8, n)) for t in range(GROUP)]
        a = [
            [
                jnp.broadcast_to(pivots[t][:, j + u : j + u + 1], (8, n)) if u >= t else None
                for u in range(GROUP)
            ]
            for t in range(GROUP)
        ]
        recip = []
        mult = [[None] * GROUP for _ in range(GROUP)]
        for t in range(GROUP):
            recip.append(1.0 / a[t][t])
            for u in range(t + 1, GROUP):
                mult[u][t] = a[t][u] * recip[t]
            for u in range(t + 1, GROUP):
                for w in range(u, GROUP):
                    a[u][w] = a[u][w] - mult[u][t] * a[t][w]
        inside = (lane >= j) & (lane < j + GROUP)
        full = []
        for t in range(GROUP):
            p = jnp.where(inside, jnp.where(lane == j + t, 1.0, 0.0), pivots[t])
            for u in range(t):
                p = p - mult[t][u] * full[u]
            full.append(p)
        for q in range(s, count):
            cur = slabs[q]
            new = jnp.where(inside, 0.0, cur)
            scaled = []
            for t in range(GROUP):
                c = jnp.broadcast_to(cur[:, j + t : j + t + 1], (8, n))
                for u in range(t):
                    c = c - scaled[u] * a[u][t]
                scaled.append(c * recip[t])
            for t in range(GROUP):
                new = new - scaled[t] * full[t]
            if q == s:
                new = jnp.where(sub >= o + GROUP, new, cur)
                for t in range(GROUP):
                    new = jnp.where(sub == o + t, full[t] * lax.rsqrt(a[t][t]), new)
            slabs[q] = new
    return slabs


def factor_kernel(core_ref, own_ref, other_ref, inv_ref, work, small_ref):
    n, half, count = PANEL, PANEL // 2, PANEL // BLOCK
    at_own = pl.multiple_of(core_ref[0] * half, half)
    at_other = pl.multiple_of((1 - core_ref[0]) * half, half)
    work[pl.ds(at_own, half), :] = own_ref[...]
    work[pl.ds(at_other, half), :] = other_ref[...]
    inv_ref[...] = jnp.zeros_like(inv_ref)
    keep = lax.broadcasted_iota(jnp.int32, (BLOCK, BLOCK), 0) >= lax.broadcasted_iota(
        jnp.int32, (BLOCK, BLOCK), 1
    )

    def step(k, _):
        at = pl.multiple_of(k * BLOCK, BLOCK)
        block = work[pl.ds(at, BLOCK), pl.ds(at, BLOCK)]
        slabs = base_inverse([block[8 * q : 8 * q + 8, :] for q in range(BLOCK // 8)])
        small_ref[...] = jnp.where(keep, jnp.concatenate(slabs, axis=0), 0.0)
        inv_ref[pl.ds(at, BLOCK), pl.ds(at, BLOCK)] = small_ref[...]
        for kk in range(count):

            @pl.when(k == kk)
            def _():
                lo, hi = kk * BLOCK, (kk + 1) * BLOCK
                small = small_ref[...]
                if kk > 0:
                    inv_ref[lo:hi, :lo] = product(small, inv_ref[lo:hi, :lo], ((1,), (0,)))
                if kk < count - 1:
                    panel = product(work[hi:, lo:hi], small, ((1,), (1,)))
                    for j in range(kk + 1, count):
                        rows = slice((j - kk - 1) * BLOCK, (j - kk) * BLOCK)
                        work[j * BLOCK :, j * BLOCK : (j + 1) * BLOCK] -= product(
                            panel[rows.start :], panel[rows], ((1,), (1,))
                        )
                    inv_ref[hi:, :hi] -= product(panel, inv_ref[lo:hi, :hi], ((1,), (0,)))

        return 0

    lax.fori_loop(0, count, step, 0)


def factor_inverse(core, own, other):
    vmem = pl.BlockSpec(memory_space=pltpu.VMEM)
    return pl.pallas_call(
        factor_kernel,
        out_shape=jax.ShapeDtypeStruct((PANEL, PANEL), jnp.float32),
        in_specs=[pl.BlockSpec(memory_space=pltpu.SMEM), vmem, vmem],
        out_specs=vmem,
        scratch_shapes=[
            pltpu.VMEM((PANEL, PANEL), jnp.float32),
            pltpu.VMEM((BLOCK, BLOCK), jnp.float32),
        ],
        compiler_params=pltpu.CompilerParams(vmem_limit_bytes=12 * 1024 * 1024),
    )(core.reshape(1), own, other)


def parts_of(x):
    high = x.astype(jnp.bfloat16)
    return high, (x - high.astype(jnp.float32)).astype(jnp.bfloat16)


def local_kernel(core_ref, own_ref, other_ref, part_ref, barrier_ref, matrix_ref, local_ref, partial_ref):
    half = own_ref.shape[0]
    dims = ((1,), (1,))
    for side, ref in ((core_ref[0], own_ref), (1 - core_ref[0], other_ref)):
        cols = pl.ds(pl.multiple_of(side * half, half), half)
        scaled = ref[...] * barrier_ref[...]
        partial_ref[:, cols] = product(part_ref[...], scaled, dims)
        s_high, s_low = parts_of(scaled)
        step = 256
        for at in range(0, matrix_ref.shape[0], step):
            m_high, m_low = parts_of(matrix_ref[at : at + step, :])
            local_ref[at : at + step, cols] = (
                product(m_high, s_low, dims, None) + product(m_low, s_high, dims, None)
            ) + product(m_high, s_high, dims, None)


def local_products(core, own, other, part, barrier, matrix):
    vmem = pl.BlockSpec(memory_space=pltpu.VMEM)
    return pl.pallas_call(
        local_kernel,
        out_shape=(
            jax.ShapeDtypeStruct((matrix.shape[0], PANEL), jnp.float32),
            jax.ShapeDtypeStruct((part.shape[0], PANEL), jnp.float32),
        ),
        in_specs=[pl.BlockSpec(memory_space=pltpu.SMEM)] + [vmem] * 5,
        out_specs=(vmem, vmem),
        compiler_params=pltpu.CompilerParams(vmem_limit_bytes=16 * 1024 * 1024),
    )(core.reshape(1), own, other, part, barrier.reshape(1, -1), matrix)


def swap(x):
    return lax.ppermute(x, "c", [(0, 1), (1, 0)])


def body(matrix, barrier, panel_index, row_offset):
    nz, nx, ny = lax.axis_size("z"), lax.axis_size("x"), lax.axis_size("y")
    z, c, x, y = (lax.axis_index(name) for name in ("z", "c", "x", "y"))
    rows_here = matrix.shape[0]
    half = PANEL // 2
    chunk = half // nz
    first = panel_index[0] * PANEL + row_offset[0]
    own_first = (2 * z + c) * rows_here
    def rows_of(side):
        wanted = first - own_first + half * side + jnp.arange(half, dtype=jnp.int32)
        inside = (wanted >= 0) & (wanted < rows_here)
        found = jnp.take(matrix, jnp.clip(wanted, 0, rows_here - 1), axis=0)
        return jnp.where(inside[:, None], found, 0.0)

    mine = rows_of(c) + swap(rows_of(1 - c))
    part = lax.all_to_all(mine.reshape(nz, chunk, -1), "z", 0, 0, tiled=True).sum(0)
    gathered = lax.all_to_all(
        jnp.broadcast_to(part[None], (nz,) + part.shape), "z", 0, 0, tiled=True
    ).reshape(half, -1)
    local, partial = local_products(c, gathered, swap(gathered), part, barrier, matrix)
    summed = lax.psum_scatter(local, "x", scatter_dimension=0, tiled=True)
    row = lax.all_to_all(partial.reshape(chunk, 1, PANEL), ("x", "y"), 0, 0, tiled=True).sum(0)
    row_id = half * c + chunk * z + ny * x + y
    row = row + (jnp.arange(PANEL, dtype=jnp.int32) == row_id).astype(jnp.float32)[None, :]
    own = lax.all_to_all(
        jnp.broadcast_to(row[None], (nz * nx * ny, 1, PANEL)), ("z", "x", "y"), 0, 0, tiled=True
    )
    own, summed = lax.optimization_barrier((own, summed))
    summed = lax.psum_scatter(summed, "y", scatter_dimension=0, tiled=True)
    own = own.reshape(half, PANEL)
    other = swap(own)
    inverse = factor_inverse(c, own, other)
    share_rows = summed.shape[0]
    ids = own_first + (ny * x + y) * share_rows + jnp.arange(share_rows, dtype=jnp.int32)
    cols = jnp.arange(PANEL, dtype=jnp.int32)
    normal = summed + (ids[:, None] == first + cols[None, :]).astype(jnp.float32)
    result = product(normal, inverse, ((1,), (1,)))
    return jnp.where((ids >= first)[:, None], result, 0.0)


def solution(mesh):
    devices = np.asarray(mesh.devices).reshape(8, 2, 4, 8)
    split = Mesh(devices, ("z", "c", "x", "y"))
    return jax.shard_map(
        body,
        mesh=split,
        in_specs=(P(("z", "c"), ("x", "y")), P(("x", "y")), P(), P()),
        out_specs=P(("z", "c", "x", "y"), None),
        check_vma=False,
    )
```

```python
import functools

import jax
import jax.numpy as jnp
import numpy as np
from jax import lax
from jax.experimental import pallas as pl
from jax.experimental.pallas import tpu as pltpu
from jax.sharding import Mesh
from jax.sharding import PartitionSpec as P

PANEL = 512
BLOCK = 128
GROUP = 8
HIGHEST = lax.Precision.HIGHEST


def product(x, y, dims, precision=HIGHEST):
    return lax.dot_general(
        x, y, (dims, ((), ())), precision=precision, preferred_element_type=jnp.float32
    )


def base_inverse(slabs):
    slabs = list(slabs)
    count = len(slabs)
    n = count * 8
    lane = lax.broadcasted_iota(jnp.int32, (8, n), 1)
    sub = lax.broadcasted_iota(jnp.int32, (8, n), 0)
    for j in range(0, n, GROUP):
        s, o = j // 8, j % 8
        top = slabs[s]
        pivots = [jnp.broadcast_to(top[o + t : o + t + 1, :], (8, n)) for t in range(GROUP)]
        a = [
            [
                jnp.broadcast_to(pivots[t][:, j + u : j + u + 1], (8, n)) if u >= t else None
                for u in range(GROUP)
            ]
            for t in range(GROUP)
        ]
        recip = []
        mult = [[None] * GROUP for _ in range(GROUP)]
        for t in range(GROUP):
            recip.append(1.0 / a[t][t])
            for u in range(t + 1, GROUP):
                mult[u][t] = a[t][u] * recip[t]
            for u in range(t + 1, GROUP):
                for w in range(u, GROUP):
                    a[u][w] = a[u][w] - mult[u][t] * a[t][w]
        inside = (lane >= j) & (lane < j + GROUP)
        full = []
        for t in range(GROUP):
            p = jnp.where(inside, jnp.where(lane == j + t, 1.0, 0.0), pivots[t])
            for u in range(t):
                p = p - mult[t][u] * full[u]
            full.append(p)
        for q in range(s, count):
            cur = slabs[q]
            new = jnp.where(inside, 0.0, cur)
            scaled = []
            for t in range(GROUP):
                c = jnp.broadcast_to(cur[:, j + t : j + t + 1], (8, n))
                for u in range(t):
                    c = c - scaled[u] * a[u][t]
                scaled.append(c * recip[t])
            for t in range(GROUP):
                new = new - scaled[t] * full[t]
            if q == s:
                new = jnp.where(sub >= o + GROUP, new, cur)
                for t in range(GROUP):
                    new = jnp.where(sub == o + t, full[t] * lax.rsqrt(a[t][t]), new)
            slabs[q] = new
    return slabs


def factor_kernel(core_ref, own_ref, other_ref, inv_ref, work, small_ref):
    n, half, count = PANEL, PANEL // 2, PANEL // BLOCK
    at_own = pl.multiple_of(core_ref[0] * half, half)
    at_other = pl.multiple_of((1 - core_ref[0]) * half, half)
    work[pl.ds(at_own, half), :] = own_ref[...]
    work[pl.ds(at_other, half), :] = other_ref[...]
    inv_ref[...] = jnp.zeros_like(inv_ref)
    keep = lax.broadcasted_iota(jnp.int32, (BLOCK, BLOCK), 0) >= lax.broadcasted_iota(
        jnp.int32, (BLOCK, BLOCK), 1
    )

    def step(k, _):
        at = pl.multiple_of(k * BLOCK, BLOCK)
        block = work[pl.ds(at, BLOCK), pl.ds(at, BLOCK)]
        slabs = base_inverse([block[8 * q : 8 * q + 8, :] for q in range(BLOCK // 8)])
        small_ref[...] = jnp.where(keep, jnp.concatenate(slabs, axis=0), 0.0)
        inv_ref[pl.ds(at, BLOCK), pl.ds(at, BLOCK)] = small_ref[...]
        for kk in range(count):

            @pl.when(k == kk)
            def _():
                lo, hi = kk * BLOCK, (kk + 1) * BLOCK
                small = small_ref[...]
                if kk > 0:
                    inv_ref[lo:hi, :lo] = product(small, inv_ref[lo:hi, :lo], ((1,), (0,)))
                if kk < count - 1:
                    panel = product(work[hi:, lo:hi], small, ((1,), (1,)))
                    for j in range(kk + 1, count):
                        rows = slice((j - kk - 1) * BLOCK, (j - kk) * BLOCK)
                        work[j * BLOCK :, j * BLOCK : (j + 1) * BLOCK] -= product(
                            panel[rows.start :], panel[rows], ((1,), (1,))
                        )
                    inv_ref[hi:, :hi] -= product(panel, inv_ref[lo:hi, :hi], ((1,), (0,)))

        return 0

    lax.fori_loop(0, count, step, 0)


def factor_inverse(core, own, other):
    vmem = pl.BlockSpec(memory_space=pltpu.VMEM)
    return pl.pallas_call(
        factor_kernel,
        out_shape=jax.ShapeDtypeStruct((PANEL, PANEL), jnp.float32),
        in_specs=[pl.BlockSpec(memory_space=pltpu.SMEM), vmem, vmem],
        out_specs=vmem,
        scratch_shapes=[
            pltpu.VMEM((PANEL, PANEL), jnp.float32),
            pltpu.VMEM((BLOCK, BLOCK), jnp.float32),
        ],
        compiler_params=pltpu.CompilerParams(vmem_limit_bytes=8 * 1024 * 1024),
    )(core.reshape(1), own, other)


def parts_of(x):
    high = x.astype(jnp.bfloat16)
    return high, (x - high.astype(jnp.float32)).astype(jnp.bfloat16)


def local_kernel(place_ref, own_ref, other_ref, part_ref, barrier_ref, matrix_ref, partial_ref, *local_refs):
    half = own_ref.shape[0]
    count = len(local_refs)
    block = matrix_ref.shape[0] // count
    dims = ((1,), (1,))
    for side, ref in ((place_ref[0], own_ref), (1 - place_ref[0], other_ref)):
        cols = pl.ds(pl.multiple_of(side * half, half), half)
        scaled = ref[...] * barrier_ref[...]
        partial_ref[:, cols] = product(part_ref[...], scaled, dims)
        s_high, s_low = parts_of(scaled)
        for k, out in enumerate(local_refs):
            at = pl.multiple_of(lax.rem(place_ref[1] + k, count) * block, block)
            m_high, m_low = parts_of(matrix_ref[pl.ds(at, block), :])
            out[:, cols] = (
                product(m_high, s_low, dims, None) + product(m_low, s_high, dims, None)
            ) + product(m_high, s_high, dims, None)


def local_products(core, x, nx, own, other, part, barrier, matrix):
    vmem = pl.BlockSpec(memory_space=pltpu.VMEM)
    block = jax.ShapeDtypeStruct((matrix.shape[0] // nx, PANEL), jnp.float32)
    return pl.pallas_call(
        local_kernel,
        out_shape=(jax.ShapeDtypeStruct((part.shape[0], PANEL), jnp.float32),) + (block,) * nx,
        in_specs=[pl.BlockSpec(memory_space=pltpu.SMEM)] + [vmem] * 5,
        out_specs=(vmem,) * (1 + nx),
        compiler_params=pltpu.CompilerParams(vmem_limit_bytes=10 * 1024 * 1024),
    )(jnp.stack([core, x]), own, other, part, barrier.reshape(1, -1), matrix)


def swap(x):
    return lax.ppermute(x, "c", [(0, 1), (1, 0)])


def body(matrix, barrier, panel_index, row_offset):
    nz, nx, ny = lax.axis_size("z"), lax.axis_size("x"), lax.axis_size("y")
    z, c, x, y = (lax.axis_index(name) for name in ("z", "c", "x", "y"))
    rows_here = matrix.shape[0]
    half = PANEL // 2
    chunk = half // nz
    first = panel_index[0] * PANEL + row_offset[0]
    own_first = (2 * z + c) * rows_here
    def rows_of(side):
        wanted = first - own_first + half * side + jnp.arange(half, dtype=jnp.int32)
        inside = (wanted >= 0) & (wanted < rows_here)
        found = jnp.take(matrix, jnp.clip(wanted, 0, rows_here - 1), axis=0)
        return jnp.where(inside[:, None], found, 0.0)

    mine = rows_of(c) + swap(rows_of(1 - c))
    part = lax.all_to_all(mine.reshape(nz, chunk, -1), "z", 0, 0, tiled=True).sum(0)
    gathered = lax.all_to_all(
        jnp.broadcast_to(part[None], (nz,) + part.shape), "z", 0, 0, tiled=True
    ).reshape(half, -1)
    partial, *local = local_products(c, x, nx, gathered, swap(gathered), part, barrier, matrix)
    arrived = [
        lax.ppermute(local[k], "x", [(i, (i + k) % nx) for i in range(nx)]) for k in range(1, nx)
    ]
    near, far = [arrived[0], arrived[-1]], arrived[1:-1]
    row = lax.all_to_all(partial.reshape(chunk, 1, PANEL), ("x", "y"), 0, 0, tiled=True).sum(0)
    row, near = lax.optimization_barrier((row, near))
    row_id = half * c + chunk * z + ny * x + y
    row = row + (jnp.arange(PANEL, dtype=jnp.int32) == row_id).astype(jnp.float32)[None, :]
    own = lax.all_to_all(
        jnp.broadcast_to(row[None], (nz * nx * ny, 1, PANEL)), ("z", "x", "y"), 0, 0, tiled=True
    )
    own, far = lax.optimization_barrier((own, far))
    summed = lax.all_to_all(sum(near + far, local[0]).reshape(ny, -1, PANEL), "y", 0, 0, tiled=True).sum(0)
    own = own.reshape(half, PANEL)
    other = swap(own)
    inverse = factor_inverse(c, own, other)
    share_rows = summed.shape[0]
    ids = own_first + (ny * x + y) * share_rows + jnp.arange(share_rows, dtype=jnp.int32)
    cols = jnp.arange(PANEL, dtype=jnp.int32)
    normal = summed + (ids[:, None] == first + cols[None, :]).astype(jnp.float32)
    result = product(normal, inverse, ((1,), (1,)))
    return jnp.where((ids >= first)[:, None], result, 0.0)


def solution(mesh):
    devices = np.asarray(mesh.devices).reshape(8, 2, 4, 8)
    split = Mesh(devices, ("z", "c", "x", "y"))
    return jax.shard_map(
        body,
        mesh=split,
        in_specs=(P(("z", "c"), ("x", "y")), P(("x", "y")), P(), P()),
        out_specs=P(("z", "c", "x", "y"), None),
        check_vma=False,
    )
```

```python
import functools

import jax
import jax.numpy as jnp
import numpy as np
from jax import lax
from jax.experimental import pallas as pl
from jax.experimental.pallas import tpu as pltpu
from jax.sharding import Mesh
from jax.sharding import PartitionSpec as P

PANEL = 512
BLOCK = 128
GROUP = 8
PACKED = 384
HIGHEST = lax.Precision.HIGHEST


def product(x, y, dims, precision=HIGHEST):
    return lax.dot_general(
        x, y, (dims, ((), ())), precision=precision, preferred_element_type=jnp.float32
    )


def base_inverse(slabs):
    slabs = list(slabs)
    count = len(slabs)
    n = count * 8
    lane = lax.broadcasted_iota(jnp.int32, (8, n), 1)
    sub = lax.broadcasted_iota(jnp.int32, (8, n), 0)
    for j in range(0, n, GROUP):
        s, o = j // 8, j % 8
        top = slabs[s]
        pivots = [jnp.broadcast_to(top[o + t : o + t + 1, :], (8, n)) for t in range(GROUP)]
        a = [
            [
                jnp.broadcast_to(pivots[t][:, j + u : j + u + 1], (8, n)) if u >= t else None
                for u in range(GROUP)
            ]
            for t in range(GROUP)
        ]
        recip = []
        mult = [[None] * GROUP for _ in range(GROUP)]
        for t in range(GROUP):
            recip.append(1.0 / a[t][t])
            for u in range(t + 1, GROUP):
                mult[u][t] = a[t][u] * recip[t]
            for u in range(t + 1, GROUP):
                for w in range(u, GROUP):
                    a[u][w] = a[u][w] - mult[u][t] * a[t][w]
        inside = (lane >= j) & (lane < j + GROUP)
        full = []
        for t in range(GROUP):
            p = jnp.where(inside, jnp.where(lane == j + t, 1.0, 0.0), pivots[t])
            for u in range(t):
                p = p - mult[t][u] * full[u]
            full.append(p)
        for q in range(s, count):
            cur = slabs[q]
            new = jnp.where(inside, 0.0, cur)
            scaled = []
            for t in range(GROUP):
                c = jnp.broadcast_to(cur[:, j + t : j + t + 1], (8, n))
                for u in range(t):
                    c = c - scaled[u] * a[u][t]
                scaled.append(c * recip[t])
            for t in range(GROUP):
                new = new - scaled[t] * full[t]
            if q == s:
                new = jnp.where(sub >= o + GROUP, new, cur)
                for t in range(GROUP):
                    new = jnp.where(sub == o + t, full[t] * lax.rsqrt(a[t][t]), new)
            slabs[q] = new
    return slabs


def factor_kernel(core_ref, own_ref, other_ref, inv_ref, work, small_ref):
    n, half, count = PANEL, PANEL // 2, PANEL // BLOCK

    def fill(first, second):
        work[:half, :half] = first[:, :half]
        work[half:, : half // 2] = first[:, half:]
        work[half:, half // 2 :] = second[...]

    pl.when(core_ref[0] == 0)(lambda: fill(own_ref, other_ref))
    pl.when(core_ref[0] != 0)(lambda: fill(other_ref, own_ref))
    inv_ref[...] = jnp.zeros_like(inv_ref)
    keep = lax.broadcasted_iota(jnp.int32, (BLOCK, BLOCK), 0) >= lax.broadcasted_iota(
        jnp.int32, (BLOCK, BLOCK), 1
    )

    def step(k, _):
        at = pl.multiple_of(k * BLOCK, BLOCK)
        block = work[pl.ds(at, BLOCK), pl.ds(at, BLOCK)]
        slabs = base_inverse([block[8 * q : 8 * q + 8, :] for q in range(BLOCK // 8)])
        small_ref[...] = jnp.where(keep, jnp.concatenate(slabs, axis=0), 0.0)
        inv_ref[pl.ds(at, BLOCK), pl.ds(at, BLOCK)] = small_ref[...]
        for kk in range(count):

            @pl.when(k == kk)
            def _():
                lo, hi = kk * BLOCK, (kk + 1) * BLOCK
                small = small_ref[...]
                if kk > 0:
                    inv_ref[lo:hi, :lo] = product(small, inv_ref[lo:hi, :lo], ((1,), (0,)))
                if kk < count - 1:
                    panel = product(work[hi:, lo:hi], small, ((1,), (1,)))
                    for j in range(kk + 1, count):
                        rows = slice((j - kk - 1) * BLOCK, (j - kk) * BLOCK)
                        work[j * BLOCK :, j * BLOCK : (j + 1) * BLOCK] -= product(
                            panel[rows.start :], panel[rows], ((1,), (1,))
                        )
                    inv_ref[hi:, :hi] -= product(panel, inv_ref[lo:hi, :hi], ((1,), (0,)))

        return 0

    lax.fori_loop(0, count, step, 0)


def factor_inverse(core, own, other):
    vmem = pl.BlockSpec(memory_space=pltpu.VMEM)
    return pl.pallas_call(
        factor_kernel,
        out_shape=jax.ShapeDtypeStruct((PANEL, PANEL), jnp.float32),
        in_specs=[pl.BlockSpec(memory_space=pltpu.SMEM), vmem, vmem],
        out_specs=vmem,
        scratch_shapes=[
            pltpu.VMEM((PANEL, PANEL), jnp.float32),
            pltpu.VMEM((BLOCK, BLOCK), jnp.float32),
        ],
        compiler_params=pltpu.CompilerParams(vmem_limit_bytes=8 * 1024 * 1024),
    )(core.reshape(1), own, other)


def parts_of(x):
    high = x.astype(jnp.bfloat16)
    return high, (x - high.astype(jnp.float32)).astype(jnp.bfloat16)


def local_kernel(
    place_ref, own_ref, other_ref, barrier_ref, matrix_ref, partial_ref, *refs
):
    *local_refs, scaled = refs
    half = own_ref.shape[0]
    count = len(local_refs)
    block = matrix_ref.shape[0] // count
    chunk = partial_ref.shape[0]
    dims = ((1,), (1,))
    for side, ref in ((place_ref[0], own_ref), (1 - place_ref[0], other_ref)):
        rows = pl.ds(pl.multiple_of(side * half, half), half)
        scaled[rows, :] = ref[...] * barrier_ref[...]
    rows = pl.ds(pl.multiple_of(place_ref[2] * chunk, chunk), chunk)

    @pl.when(place_ref[0] == 0)
    def _():
        partial_ref[:, :half] = product(own_ref[rows, :], scaled[:half, :], dims)
        partial_ref[:, half:] = product(other_ref[rows, :], scaled[: half // 2, :], dims)

    @pl.when(place_ref[0] != 0)
    def _():
        partial_ref[...] = product(own_ref[rows, :], scaled[half // 2 :, :], dims)

    s_high, s_low = parts_of(scaled[...])
    for k, out in enumerate(local_refs):
        at = pl.multiple_of(lax.rem(place_ref[1] + k, count) * block, block)
        m_high, m_low = parts_of(matrix_ref[pl.ds(at, block), :])
        out[...] = (
            product(m_high, s_low, dims, None) + product(m_low, s_high, dims, None)
        ) + product(m_high, s_high, dims, None)


def local_products(core, x, z, nx, chunk, own, other, barrier, matrix):
    vmem = pl.BlockSpec(memory_space=pltpu.VMEM)
    block = jax.ShapeDtypeStruct((matrix.shape[0] // nx, PANEL), jnp.float32)
    return pl.pallas_call(
        local_kernel,
        out_shape=(jax.ShapeDtypeStruct((chunk, PACKED), jnp.float32),) + (block,) * nx,
        in_specs=[pl.BlockSpec(memory_space=pltpu.SMEM)] + [vmem] * 4,
        out_specs=(vmem,) * (1 + nx),
        scratch_shapes=[pltpu.VMEM((PANEL, matrix.shape[1]), jnp.float32)],
        compiler_params=pltpu.CompilerParams(vmem_limit_bytes=14 * 1024 * 1024),
    )(jnp.stack([core, x, z]), own, other, barrier.reshape(1, -1), matrix)


def swap(x):
    return lax.ppermute(x, "c", [(0, 1), (1, 0)])


def body(matrix, barrier, panel_index, row_offset):
    nz, nx, ny = lax.axis_size("z"), lax.axis_size("x"), lax.axis_size("y")
    z, c, x, y = (lax.axis_index(name) for name in ("z", "c", "x", "y"))
    rows_here = matrix.shape[0]
    half = PANEL // 2
    chunk = half // nz
    first = panel_index[0] * PANEL + row_offset[0]
    own_first = (2 * z + c) * rows_here
    def rows_of(side):
        wanted = first - own_first + half * side + jnp.arange(half, dtype=jnp.int32)
        inside = (wanted >= 0) & (wanted < rows_here)
        found = jnp.take(matrix, jnp.clip(wanted, 0, rows_here - 1), axis=0)
        return jnp.where(inside[:, None], found, 0.0)

    mine = rows_of(c) + swap(rows_of(1 - c))
    part = lax.all_to_all(mine.reshape(nz, chunk, -1), "z", 0, 0, tiled=True).sum(0)
    gathered = lax.all_to_all(
        jnp.broadcast_to(part[None], (nz,) + part.shape), "z", 0, 0, tiled=True
    ).reshape(half, -1)
    partial, *local = local_products(
        c, x, z, nx, chunk, gathered, swap(gathered), barrier, matrix
    )
    arrived = [
        lax.ppermute(local[k], "x", [(i, (i + k) % nx) for i in range(nx)]) for k in range(1, nx)
    ]
    near, far = [arrived[0], arrived[-1]], arrived[1:-1]
    row = lax.all_to_all(partial.reshape(chunk, 1, PACKED), ("x", "y"), 0, 0, tiled=True).sum(0)
    row, far = lax.optimization_barrier((row, far))
    diagonal = chunk * z + ny * x + y + (PACKED - half) * c
    row = row + (jnp.arange(PACKED, dtype=jnp.int32) == diagonal).astype(jnp.float32)[None, :]
    own = lax.all_to_all(
        jnp.broadcast_to(row[None], (nz * nx * ny, 1, PACKED)), ("z", "x", "y"), 0, 0, tiled=True
    )
    own, near = lax.optimization_barrier((own, near))
    summed = lax.all_to_all(
        sum(near + far, local[0]).reshape(ny, -1, PANEL), "y", 0, 0, tiled=True
    ).sum(0)
    own = own.reshape(half, PACKED)
    other = swap(own)
    inverse = factor_inverse(c, own, other)
    share_rows = summed.shape[0]
    ids = own_first + (ny * x + y) * share_rows + jnp.arange(share_rows, dtype=jnp.int32)
    cols = jnp.arange(PANEL, dtype=jnp.int32)
    normal = summed + (ids[:, None] == first + cols[None, :]).astype(jnp.float32)
    result = product(normal, inverse, ((1,), (1,)))
    return jnp.where((ids >= first)[:, None], result, 0.0)


def solution(mesh):
    devices = np.asarray(mesh.devices).reshape(8, 2, 4, 8)
    split = Mesh(devices, ("z", "c", "x", "y"))
    return jax.shard_map(
        body,
        mesh=split,
        in_specs=(P(("z", "c"), ("x", "y")), P(("x", "y")), P(), P()),
        out_specs=P(("z", "c", "x", "y"), None),
        check_vma=False,
    )
```

```python
import functools

import jax
import jax.numpy as jnp
import numpy as np
from jax import lax
from jax.experimental import pallas as pl
from jax.experimental.pallas import tpu as pltpu
from jax.sharding import Mesh
from jax.sharding import PartitionSpec as P

PANEL = 512
BLOCK = 128
GROUP = 8
PACKED = 384
RING = 4
HIGHEST = lax.Precision.HIGHEST


def product(x, y, dims, precision=HIGHEST):
    return lax.dot_general(
        x, y, (dims, ((), ())), precision=precision, preferred_element_type=jnp.float32
    )


def base_inverse(slabs):
    slabs = list(slabs)
    count = len(slabs)
    n = count * 8
    lane = lax.broadcasted_iota(jnp.int32, (8, n), 1)
    sub = lax.broadcasted_iota(jnp.int32, (8, n), 0)
    for j in range(0, n, GROUP):
        s, o = j // 8, j % 8
        top = slabs[s]
        pivots = [jnp.broadcast_to(top[o + t : o + t + 1, :], (8, n)) for t in range(GROUP)]
        a = [
            [
                jnp.broadcast_to(pivots[t][:, j + u : j + u + 1], (8, n)) if u >= t else None
                for u in range(GROUP)
            ]
            for t in range(GROUP)
        ]
        recip = []
        mult = [[None] * GROUP for _ in range(GROUP)]
        for t in range(GROUP):
            recip.append(1.0 / a[t][t])
            for u in range(t + 1, GROUP):
                mult[u][t] = a[t][u] * recip[t]
            for u in range(t + 1, GROUP):
                for w in range(u, GROUP):
                    a[u][w] = a[u][w] - mult[u][t] * a[t][w]
        inside = (lane >= j) & (lane < j + GROUP)
        full = []
        for t in range(GROUP):
            p = jnp.where(inside, jnp.where(lane == j + t, 1.0, 0.0), pivots[t])
            for u in range(t):
                p = p - mult[t][u] * full[u]
            full.append(p)
        for q in range(s, count):
            cur = slabs[q]
            new = jnp.where(inside, 0.0, cur)
            scaled = []
            for t in range(GROUP):
                c = jnp.broadcast_to(cur[:, j + t : j + t + 1], (8, n))
                for u in range(t):
                    c = c - scaled[u] * a[u][t]
                scaled.append(c * recip[t])
            for t in range(GROUP):
                new = new - scaled[t] * full[t]
            if q == s:
                new = jnp.where(sub >= o + GROUP, new, cur)
                for t in range(GROUP):
                    new = jnp.where(sub == o + t, full[t] * lax.rsqrt(a[t][t]), new)
            slabs[q] = new
    return slabs


def factor_kernel(core_ref, own_ref, other_ref, inv_ref, work, small_ref):
    n, half, count = PANEL, PANEL // 2, PANEL // BLOCK

    def fill(first, second):
        work[:half, :half] = first[:, :half]
        work[half:, : half // 2] = first[:, half:]
        work[half:, half // 2 :] = second[...]

    pl.when(core_ref[0] == 0)(lambda: fill(own_ref, other_ref))
    pl.when(core_ref[0] != 0)(lambda: fill(other_ref, own_ref))
    inv_ref[...] = jnp.zeros_like(inv_ref)
    keep = lax.broadcasted_iota(jnp.int32, (BLOCK, BLOCK), 0) >= lax.broadcasted_iota(
        jnp.int32, (BLOCK, BLOCK), 1
    )

    def step(k, _):
        at = pl.multiple_of(k * BLOCK, BLOCK)
        block = work[pl.ds(at, BLOCK), pl.ds(at, BLOCK)]
        slabs = base_inverse([block[8 * q : 8 * q + 8, :] for q in range(BLOCK // 8)])
        small_ref[...] = jnp.where(keep, jnp.concatenate(slabs, axis=0), 0.0)
        inv_ref[pl.ds(at, BLOCK), pl.ds(at, BLOCK)] = small_ref[...]
        for kk in range(count):

            @pl.when(k == kk)
            def _():
                lo, hi = kk * BLOCK, (kk + 1) * BLOCK
                small = small_ref[...]
                if kk > 0:
                    inv_ref[lo:hi, :lo] = product(small, inv_ref[lo:hi, :lo], ((1,), (0,)))
                if kk < count - 1:
                    panel = product(work[hi:, lo:hi], small, ((1,), (1,)))
                    for j in range(kk + 1, count):
                        rows = slice((j - kk - 1) * BLOCK, (j - kk) * BLOCK)
                        work[j * BLOCK :, j * BLOCK : (j + 1) * BLOCK] -= product(
                            panel[rows.start :], panel[rows], ((1,), (1,))
                        )
                    inv_ref[hi:, :hi] -= product(panel, inv_ref[lo:hi, :hi], ((1,), (0,)))

        return 0

    lax.fori_loop(0, count, step, 0)


def factor_inverse(core, own, other):
    vmem = pl.BlockSpec(memory_space=pltpu.VMEM)
    return pl.pallas_call(
        factor_kernel,
        out_shape=jax.ShapeDtypeStruct((PANEL, PANEL), jnp.float32),
        in_specs=[pl.BlockSpec(memory_space=pltpu.SMEM), vmem, vmem],
        out_specs=vmem,
        scratch_shapes=[
            pltpu.VMEM((PANEL, PANEL), jnp.float32),
            pltpu.VMEM((BLOCK, BLOCK), jnp.float32),
        ],
        compiler_params=pltpu.CompilerParams(vmem_limit_bytes=8 * 1024 * 1024),
    )(core.reshape(1), own, other)


def parts_of(x):
    high = x.astype(jnp.bfloat16)
    return high, (x - high.astype(jnp.float32)).astype(jnp.bfloat16)


def local_kernel(
    place_ref, own_ref, other_ref, barrier_ref, matrix_ref, partial_ref, *refs
):
    here, to_after, far_top, far_low, to_before, scaled = refs
    half = own_ref.shape[0]
    block = matrix_ref.shape[0] // RING
    cut = block // 2
    dims = ((1,), (1,))
    for side, ref in ((place_ref[0], own_ref), (1 - place_ref[0], other_ref)):
        rows = pl.ds(pl.multiple_of(side * half, half), half)
        scaled[rows, :] = ref[...] * barrier_ref[...]

    @pl.when(place_ref[0] == 0)
    def _():
        partial_ref[:, :half] = product(own_ref[...], scaled[:half, :], dims)
        partial_ref[:, half:] = product(other_ref[...], scaled[: half // 2, :], dims)

    @pl.when(place_ref[0] != 0)
    def _():
        partial_ref[...] = product(own_ref[...], scaled[half // 2 :, :], dims)

    s_high, s_low = parts_of(scaled[...])
    for out, step, skip in (
        (far_top, 2, 0),
        (far_low, 2, cut),
        (to_after, 1, 0),
        (to_before, 3, 0),
        (here, 0, 0),
    ):
        at = pl.multiple_of(lax.rem(place_ref[1] + step, RING) * block, block)
        m_high, m_low = parts_of(matrix_ref[pl.ds(at + skip, out.shape[0]), :])
        out[...] = (
            product(m_high, s_low, dims, None) + product(m_low, s_high, dims, None)
        ) + product(m_high, s_high, dims, None)


def local_products(core, x, own, other, barrier, matrix):
    vmem = pl.BlockSpec(memory_space=pltpu.VMEM)
    block = jax.ShapeDtypeStruct((matrix.shape[0] // RING, PANEL), jnp.float32)
    cut = jax.ShapeDtypeStruct((block.shape[0] // 2, PANEL), jnp.float32)
    packed = jax.ShapeDtypeStruct((own.shape[0], PACKED), jnp.float32)
    return pl.pallas_call(
        local_kernel,
        out_shape=(packed, block, block, cut, cut, block),
        in_specs=[pl.BlockSpec(memory_space=pltpu.SMEM)] + [vmem] * 4,
        out_specs=(vmem,) * 6,
        scratch_shapes=[pltpu.VMEM((PANEL, matrix.shape[1]), jnp.float32)],
        compiler_params=pltpu.CompilerParams(vmem_limit_bytes=14 * 1024 * 1024),
    )(jnp.stack([core, x]), own, other, barrier.reshape(1, -1), matrix)


def swap(x):
    return lax.ppermute(x, "c", [(0, 1), (1, 0)])


def body(matrix, barrier, panel_index, row_offset):
    nz, nx, ny = lax.axis_size("z"), lax.axis_size("x"), lax.axis_size("y")
    z, c, x, y = (lax.axis_index(name) for name in ("z", "c", "x", "y"))
    rows_here = matrix.shape[0]
    half = PANEL // 2
    chunk = half // nz
    first = panel_index[0] * PANEL + row_offset[0]
    own_first = (2 * z + c) * rows_here
    def rows_of(side):
        wanted = first - own_first + half * side + jnp.arange(half, dtype=jnp.int32)
        inside = (wanted >= 0) & (wanted < rows_here)
        found = jnp.take(matrix, jnp.clip(wanted, 0, rows_here - 1), axis=0)
        return jnp.where(inside[:, None], found, 0.0)

    mine = rows_of(c) + swap(rows_of(1 - c))
    part = lax.all_to_all(mine.reshape(nz, chunk, -1), "z", 0, 0, tiled=True).sum(0)
    gathered = lax.all_to_all(
        jnp.broadcast_to(part[None], (nz,) + part.shape), "z", 0, 0, tiled=True
    ).reshape(half, -1)
    partial, here, to_after, far_top, far_low, to_before = local_products(
        c, x, gathered, swap(gathered), barrier, matrix
    )
    after = [(i, (i + 1) % nx) for i in range(nx)]
    before = [(i, (i - 1) % nx) for i in range(nx)]
    relayed = (lax.ppermute(far_top, "x", after), lax.ppermute(far_low, "x", before))
    share = half // (nx * ny)
    rows = lax.all_to_all(
        partial.reshape(nx * ny, share, PACKED), ("x", "y"), 0, 0, tiled=True
    ).sum(0)
    rows, (top, low) = lax.optimization_barrier((rows, relayed))
    cut = top.shape[0]
    to_after = jnp.concatenate([to_after[:cut] + top, to_after[cut:]], axis=0)
    to_before = jnp.concatenate([to_before[:cut], to_before[cut:] + low], axis=0)
    near = (lax.ppermute(to_after, "x", after), lax.ppermute(to_before, "x", before))
    diagonal = share * (ny * x + y) + jnp.arange(share, dtype=jnp.int32) + (PACKED - half) * c
    rows = rows + (
        jnp.arange(PACKED, dtype=jnp.int32)[None, :] == diagonal[:, None]
    ).astype(jnp.float32)
    own = lax.all_to_all(
        jnp.broadcast_to(rows[None], (nx * ny,) + rows.shape), ("x", "y"), 0, 0, tiled=True
    )
    own, near = lax.optimization_barrier((own, near))
    summed = lax.all_to_all(
        (here + near[0] + near[1]).reshape(ny, -1, PANEL), "y", 0, 0, tiled=True
    ).sum(0)
    own = own.reshape(half, PACKED)
    other = swap(own)
    inverse = factor_inverse(c, own, other)
    share_rows = summed.shape[0]
    ids = own_first + (ny * x + y) * share_rows + jnp.arange(share_rows, dtype=jnp.int32)
    cols = jnp.arange(PANEL, dtype=jnp.int32)
    normal = summed + (ids[:, None] == first + cols[None, :]).astype(jnp.float32)
    result = product(normal, inverse, ((1,), (1,)))
    return jnp.where((ids >= first)[:, None], result, 0.0)


def solution(mesh):
    devices = np.asarray(mesh.devices).reshape(8, 2, 4, 8)
    split = Mesh(devices, ("z", "c", "x", "y"))
    return jax.shard_map(
        body,
        mesh=split,
        in_specs=(P(("z", "c"), ("x", "y")), P(("x", "y")), P(), P()),
        out_specs=P(("z", "c", "x", "y"), None),
        check_vma=False,
    )
```

```python
import functools

import jax
import jax.numpy as jnp
import numpy as np
from jax import lax
from jax.experimental import pallas as pl
from jax.experimental.pallas import tpu as pltpu
from jax.sharding import Mesh
from jax.sharding import PartitionSpec as P

PANEL = 512
BLOCK = 128
GROUP = 8
PACKED = 384
HIGHEST = lax.Precision.HIGHEST


def product(x, y, dims, precision=HIGHEST):
    return lax.dot_general(
        x, y, (dims, ((), ())), precision=precision, preferred_element_type=jnp.float32
    )


def base_inverse(slabs):
    slabs = list(slabs)
    count = len(slabs)
    n = count * 8
    lane = lax.broadcasted_iota(jnp.int32, (8, n), 1)
    sub = lax.broadcasted_iota(jnp.int32, (8, n), 0)
    for j in range(0, n, GROUP):
        s, o = j // 8, j % 8
        top = slabs[s]
        pivots = [jnp.broadcast_to(top[o + t : o + t + 1, :], (8, n)) for t in range(GROUP)]
        a = [
            [
                jnp.broadcast_to(pivots[t][:, j + u : j + u + 1], (8, n)) if u >= t else None
                for u in range(GROUP)
            ]
            for t in range(GROUP)
        ]
        recip = []
        mult = [[None] * GROUP for _ in range(GROUP)]
        for t in range(GROUP):
            recip.append(1.0 / a[t][t])
            for u in range(t + 1, GROUP):
                mult[u][t] = a[t][u] * recip[t]
            for u in range(t + 1, GROUP):
                for w in range(u, GROUP):
                    a[u][w] = a[u][w] - mult[u][t] * a[t][w]
        inside = (lane >= j) & (lane < j + GROUP)
        full = []
        for t in range(GROUP):
            p = jnp.where(inside, jnp.where(lane == j + t, 1.0, 0.0), pivots[t])
            for u in range(t):
                p = p - mult[t][u] * full[u]
            full.append(p)
        for q in range(s, count):
            cur = slabs[q]
            new = jnp.where(inside, 0.0, cur)
            scaled = []
            for t in range(GROUP):
                c = jnp.broadcast_to(cur[:, j + t : j + t + 1], (8, n))
                for u in range(t):
                    c = c - scaled[u] * a[u][t]
                scaled.append(c * recip[t])
            for t in range(GROUP):
                new = new - scaled[t] * full[t]
            if q == s:
                new = jnp.where(sub >= o + GROUP, new, cur)
                for t in range(GROUP):
                    new = jnp.where(sub == o + t, full[t] * lax.rsqrt(a[t][t]), new)
            slabs[q] = new
    return slabs


def factor_kernel(core_ref, own_ref, other_ref, inv_ref, work, small_ref):
    n, half, count = PANEL, PANEL // 2, PANEL // BLOCK

    def fill(first, second):
        work[:half, :half] = first[:, :half]
        work[half:, : half // 2] = first[:, half:]
        work[half:, half // 2 :] = second[...]

    pl.when(core_ref[0] == 0)(lambda: fill(own_ref, other_ref))
    pl.when(core_ref[0] != 0)(lambda: fill(other_ref, own_ref))
    inv_ref[...] = jnp.zeros_like(inv_ref)
    keep = lax.broadcasted_iota(jnp.int32, (BLOCK, BLOCK), 0) >= lax.broadcasted_iota(
        jnp.int32, (BLOCK, BLOCK), 1
    )

    def step(k, _):
        at = pl.multiple_of(k * BLOCK, BLOCK)
        block = work[pl.ds(at, BLOCK), pl.ds(at, BLOCK)]
        slabs = base_inverse([block[8 * q : 8 * q + 8, :] for q in range(BLOCK // 8)])
        small_ref[...] = jnp.where(keep, jnp.concatenate(slabs, axis=0), 0.0)
        inv_ref[pl.ds(at, BLOCK), pl.ds(at, BLOCK)] = small_ref[...]
        for kk in range(count):

            @pl.when(k == kk)
            def _():
                lo, hi = kk * BLOCK, (kk + 1) * BLOCK
                small = small_ref[...]
                if kk > 0:
                    inv_ref[lo:hi, :lo] = product(small, inv_ref[lo:hi, :lo], ((1,), (0,)))
                if kk < count - 1:
                    panel = product(work[hi:, lo:hi], small, ((1,), (1,)))
                    for j in range(kk + 1, count):
                        rows = slice((j - kk - 1) * BLOCK, (j - kk) * BLOCK)
                        work[j * BLOCK :, j * BLOCK : (j + 1) * BLOCK] -= product(
                            panel[rows.start :], panel[rows], ((1,), (1,))
                        )
                    inv_ref[hi:, :hi] -= product(panel, inv_ref[lo:hi, :hi], ((1,), (0,)))

        return 0

    lax.fori_loop(0, count, step, 0)


def factor_inverse(core, own, other):
    vmem = pl.BlockSpec(memory_space=pltpu.VMEM)
    return pl.pallas_call(
        factor_kernel,
        out_shape=jax.ShapeDtypeStruct((PANEL, PANEL), jnp.float32),
        in_specs=[pl.BlockSpec(memory_space=pltpu.SMEM), vmem, vmem],
        out_specs=vmem,
        scratch_shapes=[
            pltpu.VMEM((PANEL, PANEL), jnp.float32),
            pltpu.VMEM((BLOCK, BLOCK), jnp.float32),
        ],
        compiler_params=pltpu.CompilerParams(vmem_limit_bytes=8 * 1024 * 1024),
    )(core.reshape(1), own, other)


def pick_kernel(place_ref, matrix_ref, mine_ref, theirs_ref):
    half, total = mine_ref.shape[0], matrix_ref.shape[0]
    for side, out in ((place_ref[0], mine_ref), (1 - place_ref[0], theirs_ref)):
        start = place_ref[1] + side * half

        @pl.when((start > -half) & (start < total))
        def _():
            def copy(i, _):
                row = start + i
                found = matrix_ref[pl.ds(jnp.clip(row, 0, total - 1), 1), :]
                out[pl.ds(i, 1), :] = jnp.where((row >= 0) & (row < total), found, 0.0)
                return 0

            lax.fori_loop(0, half, copy, 0, unroll=8)

        @pl.when((start <= -half) | (start >= total))
        def _():
            out[...] = jnp.zeros_like(out)


def pick_rows(core, start, matrix):
    vmem = pl.BlockSpec(memory_space=pltpu.VMEM)
    half = jax.ShapeDtypeStruct((PANEL // 2, matrix.shape[1]), jnp.float32)
    return pl.pallas_call(
        pick_kernel,
        out_shape=(half, half),
        in_specs=[pl.BlockSpec(memory_space=pltpu.SMEM), vmem],
        out_specs=(vmem, vmem),
        compiler_params=pltpu.CompilerParams(vmem_limit_bytes=14 * 1024 * 1024),
    )(jnp.stack([core, start]), matrix)


def parts_of(x):
    high = x.astype(jnp.bfloat16)
    return high, (x - high.astype(jnp.float32)).astype(jnp.bfloat16)


def local_kernel(
    place_ref, own_ref, other_ref, barrier_ref, matrix_ref, partial_ref, *refs
):
    *local_refs, scaled = refs
    half = own_ref.shape[0]
    count = len(local_refs)
    block = matrix_ref.shape[0] // count
    chunk = partial_ref.shape[0]
    dims = ((1,), (1,))
    for side, ref in ((place_ref[0], own_ref), (1 - place_ref[0], other_ref)):
        rows = pl.ds(pl.multiple_of(side * half, half), half)
        scaled[rows, :] = ref[...] * barrier_ref[...]
    rows = pl.ds(pl.multiple_of(place_ref[2] * chunk, chunk), chunk)

    @pl.when(place_ref[0] == 0)
    def _():
        partial_ref[:, :half] = product(own_ref[rows, :], scaled[:half, :], dims)
        partial_ref[:, half:] = product(other_ref[rows, :], scaled[: half // 2, :], dims)

    @pl.when(place_ref[0] != 0)
    def _():
        partial_ref[...] = product(own_ref[rows, :], scaled[half // 2 :, :], dims)

    s_high, s_low = parts_of(scaled[...])
    for k, out in enumerate(local_refs):
        at = pl.multiple_of(lax.rem(place_ref[1] + k, count) * block, block)
        m_high, m_low = parts_of(matrix_ref[pl.ds(at, block), :])
        out[...] = (
            product(m_high, s_low, dims, None) + product(m_low, s_high, dims, None)
        ) + product(m_high, s_high, dims, None)


def local_products(core, x, z, nx, chunk, own, other, barrier, matrix):
    vmem = pl.BlockSpec(memory_space=pltpu.VMEM)
    block = jax.ShapeDtypeStruct((matrix.shape[0] // nx, PANEL), jnp.float32)
    return pl.pallas_call(
        local_kernel,
        out_shape=(jax.ShapeDtypeStruct((chunk, PACKED), jnp.float32),) + (block,) * nx,
        in_specs=[pl.BlockSpec(memory_space=pltpu.SMEM)] + [vmem] * 4,
        out_specs=(vmem,) * (1 + nx),
        scratch_shapes=[pltpu.VMEM((PANEL, matrix.shape[1]), jnp.float32)],
        compiler_params=pltpu.CompilerParams(vmem_limit_bytes=14 * 1024 * 1024),
    )(jnp.stack([core, x, z]), own, other, barrier.reshape(1, -1), matrix)


def swap(x):
    return lax.ppermute(x, "c", [(0, 1), (1, 0)])


def body(matrix, barrier, panel_index, row_offset):
    nz, nx, ny = lax.axis_size("z"), lax.axis_size("x"), lax.axis_size("y")
    z, c, x, y = (lax.axis_index(name) for name in ("z", "c", "x", "y"))
    rows_here = matrix.shape[0]
    half = PANEL // 2
    chunk = half // nz
    first = panel_index[0] * PANEL + row_offset[0]
    own_first = (2 * z + c) * rows_here
    mine, theirs = pick_rows(c, first - own_first, matrix)
    mine = mine + swap(theirs)
    part = lax.all_to_all(mine.reshape(nz, chunk, -1), "z", 0, 0, tiled=True).sum(0)
    gathered = lax.all_to_all(
        jnp.broadcast_to(part[None], (nz,) + part.shape), "z", 0, 0, tiled=True
    ).reshape(half, -1)
    partial, *local = local_products(
        c, x, z, nx, chunk, gathered, swap(gathered), barrier, matrix
    )
    arrived = [
        lax.ppermute(local[k], "x", [(i, (i + k) % nx) for i in range(nx)]) for k in range(1, nx)
    ]
    near, far = [arrived[0], arrived[-1]], arrived[1:-1]
    row = lax.all_to_all(partial.reshape(chunk, 1, PACKED), ("x", "y"), 0, 0, tiled=True).sum(0)
    row, far = lax.optimization_barrier((row, far))
    diagonal = chunk * z + ny * x + y + (PACKED - half) * c
    row = row + (jnp.arange(PACKED, dtype=jnp.int32) == diagonal).astype(jnp.float32)[None, :]
    own = lax.all_to_all(
        jnp.broadcast_to(row[None], (nz * nx * ny, 1, PACKED)), ("z", "x", "y"), 0, 0, tiled=True
    )
    own, near = lax.optimization_barrier((own, near))
    summed = lax.all_to_all(
        sum(near + far, local[0]).reshape(ny, -1, PANEL), "y", 0, 0, tiled=True
    ).sum(0)
    own = own.reshape(half, PACKED)
    other = swap(own)
    inverse = factor_inverse(c, own, other)
    share_rows = summed.shape[0]
    ids = own_first + (ny * x + y) * share_rows + jnp.arange(share_rows, dtype=jnp.int32)
    cols = jnp.arange(PANEL, dtype=jnp.int32)
    normal = summed + (ids[:, None] == first + cols[None, :]).astype(jnp.float32)
    result = product(normal, inverse, ((1,), (1,)))
    return jnp.where((ids >= first)[:, None], result, 0.0)


def solution(mesh):
    devices = np.asarray(mesh.devices).reshape(8, 2, 4, 8)
    split = Mesh(devices, ("z", "c", "x", "y"))
    return jax.shard_map(
        body,
        mesh=split,
        in_specs=(P(("z", "c"), ("x", "y")), P(("x", "y")), P(), P()),
        out_specs=P(("z", "c", "x", "y"), None),
        check_vma=False,
    )
```

```python
import functools

import jax
import jax.numpy as jnp
import numpy as np
from jax import lax
from jax.experimental import pallas as pl
from jax.experimental.pallas import tpu as pltpu
from jax.sharding import Mesh
from jax.sharding import PartitionSpec as P

PANEL = 512
BLOCK = 128
GROUP = 8
PACKED = 384
HIGHEST = lax.Precision.HIGHEST


def product(x, y, dims, precision=HIGHEST):
    return lax.dot_general(
        x, y, (dims, ((), ())), precision=precision, preferred_element_type=jnp.float32
    )


def base_inverse(slabs):
    slabs = list(slabs)
    count = len(slabs)
    n = count * 8
    lane = lax.broadcasted_iota(jnp.int32, (8, n), 1)
    sub = lax.broadcasted_iota(jnp.int32, (8, n), 0)
    for j in range(0, n, GROUP):
        s, o = j // 8, j % 8
        top = slabs[s]
        pivots = [jnp.broadcast_to(top[o + t : o + t + 1, :], (8, n)) for t in range(GROUP)]
        a = [
            [
                jnp.broadcast_to(pivots[t][:, j + u : j + u + 1], (8, n)) if u >= t else None
                for u in range(GROUP)
            ]
            for t in range(GROUP)
        ]
        recip = []
        mult = [[None] * GROUP for _ in range(GROUP)]
        for t in range(GROUP):
            recip.append(1.0 / a[t][t])
            for u in range(t + 1, GROUP):
                mult[u][t] = a[t][u] * recip[t]
            for u in range(t + 1, GROUP):
                for w in range(u, GROUP):
                    a[u][w] = a[u][w] - mult[u][t] * a[t][w]
        inside = (lane >= j) & (lane < j + GROUP)
        full = []
        for t in range(GROUP):
            p = jnp.where(inside, jnp.where(lane == j + t, 1.0, 0.0), pivots[t])
            for u in range(t):
                p = p - mult[t][u] * full[u]
            full.append(p)
        for q in range(s, count):
            cur = slabs[q]
            new = jnp.where(inside, 0.0, cur)
            scaled = []
            for t in range(GROUP):
                c = jnp.broadcast_to(cur[:, j + t : j + t + 1], (8, n))
                for u in range(t):
                    c = c - scaled[u] * a[u][t]
                scaled.append(c * recip[t])
            for t in range(GROUP):
                new = new - scaled[t] * full[t]
            if q == s:
                new = jnp.where(sub >= o + GROUP, new, cur)
                for t in range(GROUP):
                    new = jnp.where(sub == o + t, full[t] * lax.rsqrt(a[t][t]), new)
            slabs[q] = new
    return slabs


def factor_kernel(core_ref, own_ref, other_ref, inv_ref, work, small_ref):
    n, half, count = PANEL, PANEL // 2, PANEL // BLOCK

    def fill(first, second):
        work[:half, :half] = first[:, :half]
        work[half:, : half // 2] = first[:, half:]
        work[half:, half // 2 :] = second[...]

    pl.when(core_ref[0] == 0)(lambda: fill(own_ref, other_ref))
    pl.when(core_ref[0] != 0)(lambda: fill(other_ref, own_ref))
    inv_ref[...] = jnp.zeros_like(inv_ref)
    keep = lax.broadcasted_iota(jnp.int32, (BLOCK, BLOCK), 0) >= lax.broadcasted_iota(
        jnp.int32, (BLOCK, BLOCK), 1
    )

    def step(k, _):
        at = pl.multiple_of(k * BLOCK, BLOCK)
        block = work[pl.ds(at, BLOCK), pl.ds(at, BLOCK)]
        slabs = base_inverse([block[8 * q : 8 * q + 8, :] for q in range(BLOCK // 8)])
        small_ref[...] = jnp.where(keep, jnp.concatenate(slabs, axis=0), 0.0)
        inv_ref[pl.ds(at, BLOCK), pl.ds(at, BLOCK)] = small_ref[...]
        for kk in range(count):

            @pl.when(k == kk)
            def _():
                lo, hi = kk * BLOCK, (kk + 1) * BLOCK
                small = small_ref[...]
                if kk > 0:
                    inv_ref[lo:hi, :lo] = product(small, inv_ref[lo:hi, :lo], ((1,), (0,)))
                if kk < count - 1:
                    panel = product(work[hi:, lo:hi], small, ((1,), (1,)))
                    for j in range(kk + 1, count):
                        rows = slice((j - kk - 1) * BLOCK, (j - kk) * BLOCK)
                        work[j * BLOCK :, j * BLOCK : (j + 1) * BLOCK] -= product(
                            panel[rows.start :], panel[rows], ((1,), (1,))
                        )
                    inv_ref[hi:, :hi] -= product(panel, inv_ref[lo:hi, :hi], ((1,), (0,)))

        return 0

    lax.fori_loop(0, count, step, 0)


def factor_inverse(core, own, other):
    vmem = pl.BlockSpec(memory_space=pltpu.VMEM)
    return pl.pallas_call(
        factor_kernel,
        out_shape=jax.ShapeDtypeStruct((PANEL, PANEL), jnp.float32),
        in_specs=[pl.BlockSpec(memory_space=pltpu.SMEM), vmem, vmem],
        out_specs=vmem,
        scratch_shapes=[
            pltpu.VMEM((PANEL, PANEL), jnp.float32),
            pltpu.VMEM((BLOCK, BLOCK), jnp.float32),
        ],
        compiler_params=pltpu.CompilerParams(vmem_limit_bytes=8 * 1024 * 1024),
    )(core.reshape(1), own, other)


def pick_kernel(place_ref, matrix_ref, mine_ref, theirs_ref):
    half, total = mine_ref.shape[0], matrix_ref.shape[0]
    for side, out in ((place_ref[0], mine_ref), (1 - place_ref[0], theirs_ref)):
        start = place_ref[1] + side * half

        @pl.when((start > -half) & (start < total))
        def _():
            def copy(i, _):
                row = start + i
                found = matrix_ref[pl.ds(jnp.clip(row, 0, total - 1), 1), :]
                out[pl.ds(i, 1), :] = jnp.where((row >= 0) & (row < total), found, 0.0)
                return 0

            lax.fori_loop(0, half, copy, 0, unroll=8)

        @pl.when((start <= -half) | (start >= total))
        def _():
            out[...] = jnp.zeros_like(out)


def pick_rows(core, start, matrix):
    vmem = pl.BlockSpec(memory_space=pltpu.VMEM)
    half = jax.ShapeDtypeStruct((PANEL // 2, matrix.shape[1]), jnp.float32)
    return pl.pallas_call(
        pick_kernel,
        out_shape=(half, half),
        in_specs=[pl.BlockSpec(memory_space=pltpu.SMEM), vmem],
        out_specs=(vmem, vmem),
        compiler_params=pltpu.CompilerParams(vmem_limit_bytes=14 * 1024 * 1024),
    )(jnp.stack([core, start]), matrix)


def parts_of(x):
    high = x.astype(jnp.bfloat16)
    return high, (x - high.astype(jnp.float32)).astype(jnp.bfloat16)


def local_kernel(
    place_ref, own_ref, other_ref, barrier_ref, matrix_ref, partial_ref, *refs
):
    *local_refs, scaled = refs
    half = own_ref.shape[0]
    count = len(local_refs)
    block = matrix_ref.shape[0] // count
    chunk = partial_ref.shape[0]
    dims = ((1,), (1,))
    for side, ref in ((place_ref[0], own_ref), (1 - place_ref[0], other_ref)):
        rows = pl.ds(pl.multiple_of(side * half, half), half)
        scaled[rows, :] = ref[...] * barrier_ref[...]
    rows = pl.ds(pl.multiple_of(place_ref[2] * chunk, chunk), chunk)

    @pl.when(place_ref[0] == 0)
    def _():
        partial_ref[:, :half] = product(own_ref[rows, :], scaled[:half, :], dims)
        partial_ref[:, half:] = product(other_ref[rows, :], scaled[: half // 2, :], dims)

    @pl.when(place_ref[0] != 0)
    def _():
        partial_ref[...] = product(own_ref[rows, :], scaled[half // 2 :, :], dims)

    s_high, s_low = parts_of(scaled[...])
    for k, out in enumerate(local_refs):
        at = pl.multiple_of(lax.rem(place_ref[1] + k, count) * block, block)
        m_high, m_low = parts_of(matrix_ref[pl.ds(at, block), :])
        out[...] = (
            product(m_high, s_low, dims, None) + product(m_low, s_high, dims, None)
        ) + product(m_high, s_high, dims, None)


def local_products(core, x, z, nx, chunk, own, other, barrier, matrix):
    vmem = pl.BlockSpec(memory_space=pltpu.VMEM)
    block = jax.ShapeDtypeStruct((matrix.shape[0] // nx, PANEL), jnp.float32)
    return pl.pallas_call(
        local_kernel,
        out_shape=(jax.ShapeDtypeStruct((chunk, PACKED), jnp.float32),) + (block,) * nx,
        in_specs=[pl.BlockSpec(memory_space=pltpu.SMEM)] + [vmem] * 4,
        out_specs=(vmem,) * (1 + nx),
        scratch_shapes=[pltpu.VMEM((PANEL, matrix.shape[1]), jnp.float32)],
        compiler_params=pltpu.CompilerParams(vmem_limit_bytes=14 * 1024 * 1024),
    )(jnp.stack([core, x, z]), own, other, barrier.reshape(1, -1), matrix)


def swap(x):
    return lax.ppermute(x, "c", [(0, 1), (1, 0)])


def body(matrix, barrier, panel_index, row_offset):
    nz, nx, ny = lax.axis_size("z"), lax.axis_size("x"), lax.axis_size("y")
    z, c, x, y = (lax.axis_index(name) for name in ("z", "c", "x", "y"))
    rows_here = matrix.shape[0]
    half = PANEL // 2
    chunk = half // nz
    first = panel_index[0] * PANEL + row_offset[0]
    own_first = (2 * z + c) * rows_here
    mine, theirs = pick_rows(c, first - own_first, matrix)
    mine = mine + swap(theirs)
    part = lax.all_to_all(mine.reshape(nz, chunk, -1), "z", 0, 0, tiled=True).sum(0)
    gathered = lax.all_to_all(
        jnp.broadcast_to(part[None], (nz,) + part.shape), "z", 0, 0, tiled=True
    ).reshape(half, -1)
    partial, *local = local_products(
        c, x, z, nx, chunk, gathered, swap(gathered), barrier, matrix
    )
    arrived = [
        lax.ppermute(local[k], "x", [(i, (i + k) % nx) for i in range(nx)]) for k in range(1, nx)
    ]
    near, far = arrived[:1], arrived[1:]
    row = lax.all_to_all(partial.reshape(chunk, 1, PACKED), ("x", "y"), 0, 0, tiled=True).sum(0)
    row, far = lax.optimization_barrier((row, far))
    diagonal = chunk * z + ny * x + y + (PACKED - half) * c
    row = row + (jnp.arange(PACKED, dtype=jnp.int32) == diagonal).astype(jnp.float32)[None, :]
    own = lax.all_to_all(
        jnp.broadcast_to(row[None], (nz * nx * ny, 1, PACKED)), ("z", "x", "y"), 0, 0, tiled=True
    )
    own, near = lax.optimization_barrier((own, near))
    summed = lax.all_to_all(
        sum(near + far, local[0]).reshape(ny, -1, PANEL), "y", 0, 0, tiled=True
    ).sum(0)
    own = own.reshape(half, PACKED)
    other = swap(own)
    inverse = factor_inverse(c, own, other)
    share_rows = summed.shape[0]
    ids = own_first + (ny * x + y) * share_rows + jnp.arange(share_rows, dtype=jnp.int32)
    cols = jnp.arange(PANEL, dtype=jnp.int32)
    normal = summed + (ids[:, None] == first + cols[None, :]).astype(jnp.float32)
    result = product(normal, inverse, ((1,), (1,)))
    return jnp.where((ids >= first)[:, None], result, 0.0)


def solution(mesh):
    devices = np.asarray(mesh.devices).reshape(8, 2, 4, 8)
    split = Mesh(devices, ("z", "c", "x", "y"))
    return jax.shard_map(
        body,
        mesh=split,
        in_specs=(P(("z", "c"), ("x", "y")), P(("x", "y")), P(), P()),
        out_specs=P(("z", "c", "x", "y"), None),
        check_vma=False,
    )
```
